128 devices in a mesh: ind: 16 (over x, z_hi, core), bin: 8 (over z_lo, y).
Axes of the slice: x: 4, y: 4, z: 4 (z_hi: 2, z_lo: 2; z = z_hi * 2 + z_lo), core: 2. Of those that a mesh axis runs over, the one named last changes fastest.
Arguments:
- genotype: int32 [4096, 204800], P('ind', 'bin'), may hold values from 0 to 2
- snp_mean: float32 [204800], P('bin'), may hold values from 0.9 to 1.1
- snp_scale: float32 [204800], P('bin'), may hold values from 0.75 to 0.9
- snp_label: int32 [204800], P('bin'), may hold values from 0 to 23, as said below
- probe_bits: int32 [10, 4096], P(None, 'ind'), may hold values from 0 to 1
- phenotype: bfloat16 [4096], P('ind'), may hold values from -6 to 6
Outputs:
- field: bfloat16 [24, 10, 4096], P('bin', None, 'ind')
- pair: float32 [24, 24], P('bin')
- trace: float32 [24], P('bin')
- quadratic: float32 [24], P('bin')
The draws below stay inside these ranges and needn't reach their ends.
Inputs may be any that keep to these rules, and one draw needn't show every extreme that they name: `snp_label`: the label of SNP m lies from (m // 25600) * 3 to (m // 25600) * 3 + 2, and every bin holds at least one SNP.
All inputs are finite; a program needn't handle non-finite values.
Results may differ from the reference program's by a relative error of at most 0.0053.
Values may be sent and summed in bfloat16 or wider, within the bound.
A program may use at most 128 MiB of HBM per device.

```python
import jax
import jax.numpy as jnp
from jax import lax

BINS = 24
PROBES = 10
SNP_DEV = 25600
BINS_DEV = 3
INDIVIDUALS = 4096
SNPS = 204800
N_BIN = 8


def draw_snp_label(key, part):
    key = jax.random.fold_in(key, 7)
    key_local, key_offset = jax.random.split(key)
    local = jax.random.randint(key_local, (N_BIN, SNP_DEV), 0, BINS_DEV).astype(jnp.int32)
    offset = jax.random.randint(key_offset, (N_BIN, 1), 0, SNP_DEV - BINS_DEV + 1).astype(jnp.int32)
    place = jnp.arange(SNP_DEV, dtype=jnp.int32)[None, :] - offset
    local = jnp.where((place >= 0) & (place < BINS_DEV), place, local)
    labels = local + jnp.arange(N_BIN, dtype=jnp.int32)[:, None] * BINS_DEV
    return labels.reshape(SNPS).astype(jnp.int32)


def set_ends(result, rng, low, largest):
    longest = result.shape.index(max(result.shape))
    spots = []
    for shift in (0, 1):
        where = [jax.random.randint(jax.random.fold_in(rng, axis), (), 0, length) for axis, length in enumerate(result.shape)]
        where[longest] = (where[longest] + shift) % result.shape[longest]
        spots.append(tuple(where))
    return result.at[spots[0]].set(low).at[spots[1]].set(largest)


def shard_levels(key, extent, cuts, smallest, top_value):
    factor_of = 1.0
    for axis_at, blocks in cuts:
        steps = jax.random.uniform(jax.random.fold_in(jax.random.fold_in(key, 6), axis_at), (blocks,), jnp.float32, smallest / len(cuts), top_value / len(cuts))
        factor_of = factor_of * jnp.repeat(jnp.exp(steps), extent[axis_at] // blocks).reshape((-1,) + (1,) * (len(extent) - 1 - axis_at))
    return factor_of


def centred(key, shape, width, most, pieces=(), kind=jnp.bfloat16):
    array = jax.random.normal(key, shape, jnp.float32) * width
    if len(pieces) > 0:
        array = shard_levels(key, shape, pieces, -0.22, 0.18) * array
    return jnp.clip(array, min=-most, max=most).astype(kind)


def setup_inputs(seed: int = 0) -> dict:
    seeds = jax.random.split(jax.random.key(seed), 7)
    genotype = set_ends(jax.random.randint(seeds[0], (INDIVIDUALS, SNPS), 0, 3), jax.random.fold_in(seeds[0], 1), 0, 2).astype(jnp.int32)
    snp_mean = jnp.clip(0.9 + 0.20000005 * jax.random.uniform(seeds[1], (SNPS,), jnp.float32) ** shard_levels(seeds[1], (SNPS,), ((0, 8),), -0.2, 0.2), 0.9, 1.1)
    snp_scale = jnp.clip(0.75 + 0.14999998 * jax.random.uniform(seeds[2], (SNPS,), jnp.float32) ** shard_levels(seeds[2], (SNPS,), ((0, 8),), -0.2, 0.2), 0.75, 0.9)
    snp_label = draw_snp_label(jax.random.fold_in(seeds[6], 71), 0)
    probe_bits = set_ends(jax.random.randint(seeds[4], (PROBES, INDIVIDUALS), 0, 2), jax.random.fold_in(seeds[4], 1), 0, 1).astype(jnp.int32)
    phenotype = centred(seeds[5], (INDIVIDUALS,), 1.0, 6.0, ((0, 16),))
    return dict(genotype=genotype, snp_mean=snp_mean, snp_scale=snp_scale, snp_label=snp_label, probe_bits=probe_bits, phenotype=phenotype)


def standardize(geno, mean, scale):
    return ((geno.astype(jnp.float32) - mean[None, :]) / scale[None, :]).astype(jnp.bfloat16)


def reference(genotype, snp_mean, snp_scale, snp_label, probe_bits, phenotype):
    probes = (2 * probe_bits - 1).astype(jnp.bfloat16)
    left = jnp.concatenate([probes, phenotype[None, :]], axis=0)
    left_wide = left.astype(jnp.float32)
    member = snp_label[None, :] == jnp.arange(BINS, dtype=jnp.int32)[:, None]
    count = jnp.sum(member.astype(jnp.float32), axis=1)

    def first_pass(block, carry):
        moments, squares = carry
        start = (block * SNP_DEV).astype(jnp.int32)
        geno = lax.dynamic_slice_in_dim(genotype, start, SNP_DEV, 1)
        mean = lax.dynamic_slice_in_dim(snp_mean, start, SNP_DEV, 0)
        scale = lax.dynamic_slice_in_dim(snp_scale, start, SNP_DEV, 0)
        stand = standardize(geno, mean, scale).astype(jnp.float32)
        part = jnp.dot(left_wide, stand, precision=lax.Precision.HIGHEST)
        moments = lax.dynamic_update_slice_in_dim(moments, part, start, 1)
        squares = lax.dynamic_update_slice_in_dim(squares, jnp.sum(stand * stand, axis=0), start, 0)
        return moments, squares

    moments0 = jnp.zeros((PROBES + 1, SNPS), jnp.float32)
    squares0 = jnp.zeros((SNPS,), jnp.float32)
    moments, squares = lax.fori_loop(0, N_BIN, first_pass, (moments0, squares0))
    weights = lax.optimization_barrier(moments[:PROBES].astype(jnp.bfloat16)).astype(jnp.float32)

    def second_pass(block, hidden):
        start = (block * SNP_DEV).astype(jnp.int32)
        geno = lax.dynamic_slice_in_dim(genotype, start, SNP_DEV, 1)
        mean = lax.dynamic_slice_in_dim(snp_mean, start, SNP_DEV, 0)
        scale = lax.dynamic_slice_in_dim(snp_scale, start, SNP_DEV, 0)
        stand = standardize(geno, mean, scale).astype(jnp.float32)
        mask = lax.dynamic_slice_in_dim(member, start, SNP_DEV, 1)
        wblock = lax.dynamic_slice_in_dim(weights, start, SNP_DEV, 1)
        expanded = jnp.where(mask[:, None, :], wblock[None, :, :], jnp.zeros((), jnp.float32))
        expanded = expanded.reshape(BINS * PROBES, SNP_DEV)
        return hidden + jnp.dot(expanded, stand.T, precision=lax.Precision.HIGHEST)

    hidden0 = jnp.zeros((BINS * PROBES, INDIVIDUALS), jnp.float32)
    hidden = lax.fori_loop(0, N_BIN, second_pass, hidden0)
    field = (hidden.reshape(BINS, PROBES, INDIVIDUALS) / count[:, None, None]).astype(jnp.bfloat16)
    flat = lax.optimization_barrier(field).astype(jnp.float32).reshape(BINS, PROBES * INDIVIDUALS)
    pair = jnp.dot(flat, flat.T, precision=lax.Precision.HIGHEST) / (PROBES * INDIVIDUALS)
    trace = jnp.sum(jnp.where(member, squares[None, :], jnp.zeros((), jnp.float32)), axis=1) / (count * INDIVIDUALS)
    trait = moments[PROBES]
    quadratic = jnp.sum(jnp.where(member, (trait * trait)[None, :], jnp.zeros((), jnp.float32)), axis=1) / (count * INDIVIDUALS)
    return field, pair, trace, quadratic
```

```python
import functools

import jax
import jax.numpy as jnp
from jax import lax
from jax.experimental import pallas as pl
from jax.experimental.pallas import tpu as pltpu
from jax.sharding import PartitionSpec as P

BINS = 24
PROBES = 10
OWN = 3
ROWS = 256
SNPS = 25600
INDIVIDUALS = 4096
UNIT = 2048
PADDED = 26624
UNITS = 13
SUB = 256
GROUPS = ((0, 5), (5, 4), (9, 2), (11, 2))
F32 = jnp.float32
BF16 = jnp.bfloat16
MESH = pl.DeviceIdType.MESH


def split_dot(a, b):
    high = a.astype(BF16)
    low = (a - high.astype(F32)).astype(BF16)
    both = jnp.concatenate([high, low], axis=0)
    return jnp.dot(both, b, preferred_element_type=F32)


def kernel(
    geno, mean, scale, label, probes, pheno,
    field_out, pair_out, trace_out, quad_out,
    gbuf, stand, part, other, sums, arrived, weights,
    mean_v, inv_v, label_v, left_f, left_b, squares, quads, hidden, dense, fields, messages, pick,
    g_sem, s_sem, core_send, core_recv, rs_send, rs_recv, ag_send, ag_recv, half_send, half_recv,
    f_send, f_recv, m_send, m_recv,
):
    ind = lax.axis_index("ind")
    bin_ = lax.axis_index("bin")
    core = lax.rem(ind, 2)
    chip = ind // 2
    cx, cz = chip // 2, lax.rem(chip, 2)
    first = bin_ * OWN

    small = [
        pltpu.make_async_copy(mean, mean_v, s_sem.at[0]),
        pltpu.make_async_copy(scale, inv_v, s_sem.at[1]),
        pltpu.make_async_copy(label, label_v.at[:, 0:SNPS], s_sem.at[2]),
    ]
    for copy in small:
        copy.start()

    def geno_copy(u):
        at = pl.ds(pl.multiple_of(u * UNIT, UNIT), UNIT)
        return pltpu.make_async_copy(geno.at[:, at], gbuf.at[:, at], g_sem.at[u])

    last_at = pl.ds((UNITS - 1) * UNIT, SNPS - (UNITS - 1) * UNIT)
    last_copy = pltpu.make_async_copy(geno.at[:, last_at], gbuf.at[:, last_at], g_sem.at[UNITS - 1])
    for u in range(UNITS - 1):
        geno_copy(u).start()
    last_copy.start()

    barrier = pltpu.get_barrier_semaphore()
    for d in range(1, 16):
        pl.semaphore_signal(
            barrier, inc=1, device_id=(lax.rem(ind + d, 16), bin_), device_id_type=MESH
        )
    for d in range(1, 8):
        pl.semaphore_signal(
            barrier, inc=1, device_id=(ind, lax.rem(bin_ + d, 8)), device_id_type=MESH
        )

    left_f[...] = jnp.zeros_like(left_f)
    left_f[0:PROBES, :] = (2 * probes[...] - 1).astype(F32)
    left_f[PROBES : PROBES + 1, :] = pheno[...].astype(F32)
    left_b[...] = left_f[...].astype(BF16)
    part[:, SNPS:PADDED] = jnp.zeros((16, PADDED - SNPS), F32)
    label_v[:, SNPS:PADDED] = jnp.full((1, PADDED - SNPS), -1, jnp.int32)
    squares[...] = jnp.zeros_like(squares)
    quads[...] = jnp.zeros_like(quads)
    hidden[...] = jnp.zeros_like(hidden)
    for copy in small:
        copy.wait()
    inv_v[...] = 1.0 / inv_v[...]

    def moments(start, count):
        def sub(s, carry):
            off = pl.multiple_of(start + s * SUB, SUB)
            at = pl.ds(off, SUB)
            x = ((gbuf[:, at].astype(F32) - mean_v[:, at]) * inv_v[:, at]).astype(BF16)
            stand[:, at] = x
            part[:, at] = jnp.dot(left_b[...], x, preferred_element_type=F32)
            wide = x.astype(F32)
            sq = jnp.sum((wide * wide).reshape(ROWS // 8, 8, SUB), axis=0)
            lab = label_v[:, at]
            return tuple(
                carry[k] + jnp.where(lab == first + k, sq, 0.0) for k in range(OWN)
            )

        carry = lax.fori_loop(0, count, sub, tuple(squares[k] for k in range(OWN)))
        for k in range(OWN):
            squares[k] = carry[k]

    def unit_moments(u, _):
        geno_copy(u).wait()
        moments(u * UNIT, UNIT // SUB)
        return 0

    def units(lo, hi):
        lax.fori_loop(lo, min(hi, UNITS - 1), unit_moments, 0)
        if hi == UNITS:
            last_copy.wait()
            moments((UNITS - 1) * UNIT, (SNPS - (UNITS - 1) * UNIT) // SUB)

    def half_at(g, which):
        begin, n = GROUPS[g]
        half = n * UNIT // 2
        return pl.ds(pl.multiple_of(begin * UNIT + which * half, 1024), half)

    def piece_at(g, who):
        begin, n = GROUPS[g]
        half, piece = n * UNIT // 2, n * UNIT // 16
        return pl.ds(pl.multiple_of(begin * UNIT + core * half + who * piece, 128), piece)

    def partner():
        return (chip * 2 + 1 - core, bin_)

    def core_copy(g):
        at = half_at(g, 1 - core)
        return pltpu.make_async_remote_copy(
            src_ref=part.at[:, at], dst_ref=other.at[:, at],
            send_sem=core_send.at[g], recv_sem=core_recv.at[g],
            device_id=partner(), device_id_type=MESH,
        )

    hops = ((2, 1), (1, 1), (3, 1), (2, 0), (0, 1), (1, 0), (3, 0))

    def chip_at(hop):
        return lax.rem(cx + hop[0], 4) * 2 + lax.rem(cz + hop[1], 2)

    def slots(g):
        begin, n = GROUPS[g]
        return pl.ds(begin * 128, n * 128)

    def scatter(g):
        pltpu.make_async_copy(part.at[:, half_at(g, 1 - core)], other.at[:, half_at(g, core)], core_recv.at[g]).wait()
        at = half_at(g, core)
        sums[:, at] = (part[:, at] + other[:, at]).astype(BF16)
        for slot, hop in enumerate(hops):
            who = chip_at(hop)
            pltpu.make_async_remote_copy(
                src_ref=sums.at[:, piece_at(g, who)], dst_ref=arrived.at[slot, :, slots(g)],
                send_sem=rs_send.at[g], recv_sem=rs_recv.at[g],
                device_id=(who * 2 + core, bin_), device_id_type=MESH,
            ).start()

    def all_slots(g):
        return arrived.at[:, :, slots(g)]

    def gather(g):
        pltpu.make_async_copy(all_slots(g), all_slots(g), rs_recv.at[g]).wait()
        mine = piece_at(g, chip)
        total = part[:, mine] + other[:, mine]
        for slot in range(7):
            total = total + arrived[slot, :, slots(g)].astype(F32)
        weights[:, mine] = total.astype(BF16)
        for hop in hops:
            who = chip_at(hop)
            pltpu.make_async_remote_copy(
                src_ref=weights.at[:, mine], dst_ref=weights.at[:, mine],
                send_sem=ag_send.at[g], recv_sem=ag_recv.at[g],
                device_id=(who * 2 + core, bin_), device_id_type=MESH,
            ).start()
        trait = total[8:16, :]
        row = lax.broadcasted_iota(jnp.int32, trait.shape, 0)
        trait = jnp.where(row == PROBES - 8, trait * trait, 0.0)
        lab = label_v[:, mine]
        for k in range(OWN):
            own = jnp.where(lab == first + k, trait, 0.0)
            add = quads[k]
            for t in range(own.shape[1] // 128):
                add = add + own[:, t * 128 : (t + 1) * 128]
            quads[k] = add

    def seven(g):
        begin, n = GROUPS[g]
        half, piece = n * UNIT // 2, n * UNIT // 16
        return weights.at[:, pl.ds(pl.multiple_of(begin * UNIT + core * half, 1024), 7 * piece)]

    def half_copy(g):
        at = half_at(g, core)
        return pltpu.make_async_remote_copy(
            src_ref=weights.at[:, at], dst_ref=weights.at[:, at],
            send_sem=half_send.at[g], recv_sem=half_recv.at[g],
            device_id=partner(), device_id_type=MESH,
        )

    def share(g):
        pltpu.make_async_copy(seven(g), seven(g), ag_recv.at[g]).wait()
        half_copy(g).start()

    def apply(g):
        there = weights.at[:, half_at(g, 1 - core)]
        pltpu.make_async_copy(there, there, half_recv.at[g]).wait()
        begin, n = GROUPS[g]
        start = begin * UNIT
        stop = min(start + n * UNIT, SNPS)

        def sub(s, acc):
            at = pl.ds(pl.multiple_of(start + s * SUB, SUB), SUB)
            w = weights[:, at].astype(F32)
            lab = label_v[:, at]
            e = jnp.concatenate(
                [jnp.where(lab == first + k, w, 0.0).astype(BF16) for k in range(OWN)], axis=0
            )
            return acc + lax.dot_general(
                e, stand[:, at], (((1,), (1,)), ((), ())), preferred_element_type=F32
            )

        hidden[...] = lax.fori_loop(0, (stop - start) // SUB, sub, hidden[...])

    units(0, 5)
    pl.semaphore_wait(barrier, 22)
    core_copy(0).start()
    units(5, 7)
    scatter(0)
    units(7, 9)
    core_copy(1).start()
    units(9, 11)
    scatter(1)
    core_copy(2).start()
    units(11, 12)
    scatter(2)
    units(12, 13)
    core_copy(3).start()

    def pick_table():
        c = lax.broadcasted_iota(jnp.int32, (256, 128), 0)
        lane = lax.broadcasted_iota(jnp.int32, (256, 128), 1)
        inner = c & 31
        which = (c >> 5) * OWN + (inner >= 10).astype(jnp.int32) + (inner >= 20).astype(jnp.int32)
        which = jnp.where(inner < 30, which, -1000)
        for k in range(OWN):
            pick[k * 256 : (k + 1) * 256, :] = (lane == which + BINS * k).astype(F32).astype(BF16)

    pick_table()
    lab_row = label_v[:, 0:SNPS]
    counts = [
        jnp.sum((lab_row == first + k).astype(F32), axis=1, keepdims=True) for k in range(OWN)
    ]
    scatter(3)
    gather(0)
    gather(1)
    gather(2)
    gather(3)
    share(0)
    share(1)
    apply(0)
    share(2)
    apply(1)
    share(3)
    apply(2)
    apply(3)

    dense[...] = jnp.zeros_like(dense)
    for k in range(OWN):
        f = hidden[16 * k : 16 * k + PROBES, :] / counts[k]
        field_out[k] = f.astype(BF16)
        dense[PROBES * k : PROBES * (k + 1), :] = f
    fields[pl.ds(bin_, 1)] = dense[...].astype(BF16)[None]
    for d in (4, 3, 5, 2, 6, 1, 7):
        pltpu.make_async_remote_copy(
            src_ref=fields.at[bin_], dst_ref=fields.at[bin_],
            send_sem=f_send.at[0], recv_sem=f_recv.at[0],
            device_id=(ind, lax.rem(bin_ + d, 8)), device_id_type=MESH,
        ).start()

    lane = lax.broadcasted_iota(jnp.int32, (128, 128), 1)
    extra = jnp.zeros((16, 128), F32)
    for k in range(OWN):
        tr = squares[k][:, 0:128] + squares[k][:, 128:256]
        extra = extra + split_dot(tr, (lane == 72 + k).astype(F32).astype(BF16))
        extra = extra + split_dot(quads[k], (lane == 75 + k).astype(F32).astype(BF16))
    extra = extra[0:8] + extra[8:16]

    seven_fields = fields.at[0:7]
    pltpu.make_async_copy(seven_fields, seven_fields, f_recv.at[0]).wait()
    own = fields[pl.ds(bin_, 1)].reshape(32, ROWS)
    every = fields[...].reshape(256, ROWS)
    gram = lax.dot_general(own, every, (((1,), (1,)), ((), ())), preferred_element_type=F32)
    r = lax.broadcasted_iota(jnp.int32, (32, 256), 0)
    c = lax.broadcasted_iota(jnp.int32, (32, 256), 1) & 31
    rk = (r >= 10).astype(jnp.int32) + (r >= 20).astype(jnp.int32)
    ck = (c >= 10).astype(jnp.int32) + (c >= 20).astype(jnp.int32)
    gram = jnp.where(r - 10 * rk == c - 10 * ck, gram, 0.0)
    by_bin = jnp.concatenate([jnp.where(rk == k, gram, 0.0) for k in range(OWN)], axis=1)
    pairs = split_dot(by_bin, pick[...])
    message = jnp.sum(pairs.reshape(8, 8, 128), axis=0) + extra
    messages[pl.ds(ind, 1)] = message[None]
    for d in (8, 7, 9, 6, 10, 5, 11, 4, 12, 3, 13, 2, 14, 1, 15):
        pltpu.make_async_remote_copy(
            src_ref=messages.at[ind], dst_ref=messages.at[ind],
            send_sem=m_send.at[0], recv_sem=m_recv.at[0],
            device_id=(lax.rem(ind + d, 16), bin_), device_id_type=MESH,
        ).start()

    for g in range(len(GROUPS)):
        core_copy(g).wait_send()
        pltpu.make_async_copy(all_slots(g), all_slots(g), rs_send.at[g]).wait()
        pltpu.make_async_copy(seven(g), seven(g), ag_send.at[g]).wait()
        half_copy(g).wait_send()
    pltpu.make_async_copy(seven_fields, seven_fields, f_send.at[0]).wait()

    fifteen = messages.at[0:15]
    pltpu.make_async_copy(fifteen, fifteen, m_recv.at[0]).wait()
    total = messages[0]
    for i in range(1, 16):
        total = total + messages[i]
    total = jnp.sum(total, axis=0, keepdims=True)
    for k in range(OWN):
        pair_out[k : k + 1, :] = total[:, BINS * k : BINS * (k + 1)] / (PROBES * INDIVIDUALS)
        trace_out[:, k : k + 1] = total[:, 72 + k : 73 + k] / (counts[k] * INDIVIDUALS)
        quad_out[:, k : k + 1] = total[:, 75 + k : 76 + k] / (counts[k] * INDIVIDUALS)
    pltpu.make_async_copy(fifteen, fifteen, m_send.at[0]).wait()


def shards(genotype, snp_mean, snp_scale, snp_label, probe_bits, phenotype):
    anywhere = pl.BlockSpec(memory_space=pl.ANY)
    vmem = pl.BlockSpec(memory_space=pltpu.VMEM)
    dma = pltpu.SemaphoreType.DMA
    n = len(GROUPS)
    field, pair, trace, quad = pl.pallas_call(
        kernel,
        name="moments_and_fields",
        out_shape=(
            jax.ShapeDtypeStruct((OWN, PROBES, ROWS), BF16),
            jax.ShapeDtypeStruct((OWN, BINS), F32),
            jax.ShapeDtypeStruct((1, OWN), F32),
            jax.ShapeDtypeStruct((1, OWN), F32),
        ),
        in_specs=[anywhere] * 4 + [vmem] * 2,
        out_specs=(vmem,) * 4,
        scratch_shapes=[
            pltpu.VMEM((ROWS, SNPS), jnp.int32),
            pltpu.VMEM((ROWS, SNPS), BF16),
            pltpu.VMEM((16, PADDED), F32),
            pltpu.VMEM((16, PADDED), F32),
            pltpu.VMEM((16, PADDED), BF16),
            pltpu.VMEM((7, 16, PADDED // 16), BF16),
            pltpu.VMEM((16, PADDED), BF16),
            pltpu.VMEM((1, SNPS), F32),
            pltpu.VMEM((1, SNPS), F32),
            pltpu.VMEM((1, PADDED), jnp.int32),
            pltpu.VMEM((16, ROWS), F32),
            pltpu.VMEM((16, ROWS), BF16),
            pltpu.VMEM((OWN, 8, SUB), F32),
            pltpu.VMEM((OWN, 8, 128), F32),
            pltpu.VMEM((16 * OWN, ROWS), F32),
            pltpu.VMEM((32, ROWS), F32),
            pltpu.VMEM((8, 32, ROWS), BF16),
            pltpu.VMEM((16, 8, 128), F32),
            pltpu.VMEM((768, 128), BF16),
            dma((UNITS,)), dma((3,)),
            dma((n,)), dma((n,)), dma((n,)), dma((n,)), dma((n,)), dma((n,)), dma((n,)), dma((n,)),
            dma((1,)), dma((1,)), dma((1,)), dma((1,)),
        ],
        compiler_params=pltpu.CompilerParams(
            collective_id=0, has_side_effects=True, vmem_limit_bytes=58 * 2**20
        ),
        cost_estimate=pl.CostEstimate(
            flops=2 * 64 * ROWS * SNPS, bytes_accessed=4 * ROWS * SNPS, transcendentals=0
        ),
    )(
        genotype,
        snp_mean.reshape(1, -1),
        snp_scale.reshape(1, -1),
        snp_label.reshape(1, -1),
        probe_bits,
        phenotype.reshape(1, -1),
    )
    return field, pair, trace.reshape(-1), quad.reshape(-1)


def solution(mesh):
    placed = (P("ind", "bin"), P("bin"), P("bin"), P("bin"), P(None, "ind"), P("ind"))
    return jax.shard_map(
        shards,
        mesh=mesh,
        in_specs=placed,
        out_specs=(P("bin", None, "ind"), P("bin", None), P("bin"), P("bin")),
        check_vma=False,
    )
```

```python
import functools

import jax
import jax.numpy as jnp
from jax import lax
from jax.experimental import pallas as pl
from jax.experimental.pallas import tpu as pltpu
from jax.sharding import PartitionSpec as P

BINS = 24
PROBES = 10
OWN = 3
ROWS = 256
SNPS = 25600
INDIVIDUALS = 4096
UNIT = 2048
PADDED = 26624
UNITS = 13
AHEAD = 3
GROUPS = ((0, 3), (3, 3), (6, 3), (9, 2), (11, 2))
DIRECT = (2, 3, 4)
F32 = jnp.float32
BF16 = jnp.bfloat16
MESH = pl.DeviceIdType.MESH


def split_dot(a, b):
    high = a.astype(BF16)
    low = (a - high.astype(F32)).astype(BF16)
    both = jnp.concatenate([high, low], axis=0)
    return jnp.dot(both, b, preferred_element_type=F32)


def kernel(
    geno, mean, scale, label, probes, pheno,
    field_out, pair_out, trace_out, quad_out,
    gbuf, stand, part, other, sums, arrived, weights,
    mean_v, inv_v, label_v, probes_v, pheno_v, left_f, left_b, squares, quads, hidden, dense, fields, messages, pick,
    g_sem, s_sem, core_send, core_recv, rs_send, rs_recv, ag_send, ag_recv, half_send, half_recv,
    f_send, f_recv, m_send, m_recv,
):
    ind = lax.axis_index("ind")
    bin_ = lax.axis_index("bin")
    core = lax.rem(ind, 2)
    chip = ind // 2
    cx, cz = chip // 2, lax.rem(chip, 2)
    first = bin_ * OWN

    small = [
        pltpu.make_async_copy(mean, mean_v, s_sem.at[0]),
        pltpu.make_async_copy(scale, inv_v, s_sem.at[1]),
        pltpu.make_async_copy(label, label_v.at[:, 0:SNPS], s_sem.at[2]),
        pltpu.make_async_copy(probes, probes_v, s_sem.at[3]),
        pltpu.make_async_copy(pheno, pheno_v, s_sem.at[4]),
    ]
    for copy in small:
        copy.start()

    def geno_copy(u):
        at = pl.ds(pl.multiple_of(u * UNIT, UNIT), UNIT)
        return pltpu.make_async_copy(geno.at[:, at], gbuf.at[:, at], g_sem.at[u])

    last_at = pl.ds((UNITS - 1) * UNIT, SNPS - (UNITS - 1) * UNIT)
    last_copy = pltpu.make_async_copy(geno.at[:, last_at], gbuf.at[:, last_at], g_sem.at[UNITS - 1])
    for u in range(AHEAD):
        geno_copy(u).start()

    barrier = pltpu.get_barrier_semaphore()
    for d in range(1, 16):
        pl.semaphore_signal(
            barrier, inc=1, device_id=(lax.rem(ind + d, 16), bin_), device_id_type=MESH
        )
    for d in range(1, 8):
        pl.semaphore_signal(
            barrier, inc=1, device_id=(ind, lax.rem(bin_ + d, 8)), device_id_type=MESH
        )

    part[:, SNPS:PADDED] = jnp.zeros((16, PADDED - SNPS), F32)
    label_v[:, SNPS:PADDED] = jnp.full((1, PADDED - SNPS), -1, jnp.int32)
    squares[...] = jnp.zeros_like(squares)
    quads[...] = jnp.zeros_like(quads)
    hidden[...] = jnp.zeros_like(hidden)
    for copy in small:
        copy.wait()
    left_f[...] = jnp.zeros_like(left_f)
    left_f[0:PROBES, :] = (2 * probes_v[...] - 1).astype(F32)
    left_f[PROBES : PROBES + 1, :] = pheno_v[...].astype(F32).reshape(1, ROWS)
    left_b[...] = left_f[...].astype(BF16)
    inv_v[...] = 1.0 / inv_v[...]

    def fold(into, wide, lab):
        for k in range(OWN):
            own = jnp.where(lab == first + k, wide, 0.0)
            add = into[k]
            for t in range(own.shape[1] // 128):
                add = add + own[:, t * 128 : (t + 1) * 128]
            into[k] = add

    def moments(start, size):
        at = pl.ds(pl.multiple_of(start, size), size)
        x = ((gbuf[:, at].astype(F32) - mean_v[:, at]) * inv_v[:, at]).astype(BF16)
        stand[:, at] = x
        part[:, at] = jnp.dot(left_b[...], x, preferred_element_type=F32)

    def square_sums(lo, hi, size):
        def sub(s, _):
            at = pl.ds(pl.multiple_of(s * size, size), size)
            wide = stand[:, at].astype(F32)
            fold(squares, jnp.sum((wide * wide).reshape(ROWS // 8, 8, size), axis=0), label_v[:, at])
            return 0

        lax.fori_loop(lo // size, hi // size, sub, 0)

    def unit_moments(u, _):
        @pl.when(u + AHEAD < UNITS - 1)
        def _():
            geno_copy(u + AHEAD).start()

        @pl.when(u + AHEAD == UNITS - 1)
        def _():
            last_copy.start()

        geno_copy(u).wait()
        moments(u * UNIT, UNIT)
        return 0

    def units(lo, hi):
        lax.fori_loop(lo, min(hi, UNITS - 1), unit_moments, 0)
        if hi == UNITS:
            last_copy.wait()
            moments((UNITS - 1) * UNIT, SNPS - (UNITS - 1) * UNIT)

    def half_at(g, which):
        begin, n = GROUPS[g]
        half = n * UNIT // 2
        return pl.ds(pl.multiple_of(begin * UNIT + which * half, 1024), half)

    def piece_at(g, who):
        begin, n = GROUPS[g]
        half, piece = n * UNIT // 2, n * UNIT // 16
        return pl.ds(pl.multiple_of(begin * UNIT + core * half + who * piece, 128), piece)

    def partner():
        return (chip * 2 + 1 - core, bin_)

    def core_copy(g):
        at = half_at(g, 1 - core)
        return pltpu.make_async_remote_copy(
            src_ref=part.at[:, at], dst_ref=other.at[:, at],
            send_sem=core_send.at[g], recv_sem=core_recv.at[g],
            device_id=partner(), device_id_type=MESH,
        )

    hops = ((2, 1), (1, 1), (3, 1), (2, 0), (0, 1), (1, 0), (3, 0))

    def chip_at(hop):
        return lax.rem(cx + hop[0], 4) * 2 + lax.rem(cz + hop[1], 2)

    def slots(g):
        begin, n = GROUPS[g]
        return pl.ds(begin * 128, n * 128)

    def scatter(g):
        pltpu.make_async_copy(part.at[:, half_at(g, 1 - core)], other.at[:, half_at(g, core)], core_recv.at[g]).wait()
        at = half_at(g, core)
        sums[:, at] = (part[:, at] + other[:, at]).astype(BF16)
        for slot, hop in enumerate(hops):
            who = chip_at(hop)
            pltpu.make_async_remote_copy(
                src_ref=sums.at[:, piece_at(g, who)], dst_ref=arrived.at[slot, :, slots(g)],
                send_sem=rs_send.at[g], recv_sem=rs_recv.at[g],
                device_id=(who * 2 + core, bin_), device_id_type=MESH,
            ).start()

    def all_slots(g):
        return arrived.at[:, :, slots(g)]

    def gather(g):
        pltpu.make_async_copy(all_slots(g), all_slots(g), rs_recv.at[g]).wait()
        mine = piece_at(g, chip)
        total = part[:, mine] + other[:, mine]
        for slot in range(7):
            total = total + arrived[slot, :, slots(g)].astype(F32)
        weights[:, mine] = total.astype(BF16)
        targets = [chip_at(hop) * 2 + core for hop in hops]
        if g in DIRECT:
            targets = [chip_at(hop) * 2 + 1 - core for hop in hops] + targets + [chip * 2 + 1 - core]
        for target in targets:
            pltpu.make_async_remote_copy(
                src_ref=weights.at[:, mine], dst_ref=weights.at[:, mine],
                send_sem=ag_send.at[g], recv_sem=ag_recv.at[g],
                device_id=(target, bin_), device_id_type=MESH,
            ).start()
        trait = total[8:16, :]
        row = lax.broadcasted_iota(jnp.int32, trait.shape, 0)
        trait = jnp.where(row == PROBES - 8, trait * trait, 0.0)
        fold(quads, trait, label_v[:, mine])

    def gathered(g):
        begin, n = GROUPS[g]
        count = 15 if g in DIRECT else 7
        return weights.at[:, pl.ds(begin * UNIT, count * n * UNIT // 16)]

    def half_copy(g):
        at = half_at(g, core)
        return pltpu.make_async_remote_copy(
            src_ref=weights.at[:, at], dst_ref=weights.at[:, at],
            send_sem=half_send.at[g], recv_sem=half_recv.at[g],
            device_id=partner(), device_id_type=MESH,
        )

    def share(g):
        pltpu.make_async_copy(gathered(g), gathered(g), ag_recv.at[g]).wait()
        half_copy(g).start()

    def apply(g):
        if g in DIRECT:
            pltpu.make_async_copy(gathered(g), gathered(g), ag_recv.at[g]).wait()
        else:
            there = weights.at[:, half_at(g, 1 - core)]
            pltpu.make_async_copy(there, there, half_recv.at[g]).wait()
        begin, n = GROUPS[g]
        start = begin * UNIT
        stop = min(start + n * UNIT, SNPS)

        size = stop - start

        def sub(s, acc):
            at = pl.ds(pl.multiple_of(start + s * size, 1024), size)
            w = weights[:, at].astype(F32)
            lab = label_v[:, at]
            e = jnp.concatenate(
                [jnp.where(lab == first + k, w, 0.0).astype(BF16) for k in range(OWN)], axis=0
            )
            return acc + lax.dot_general(
                e, stand[:, at], (((1,), (1,)), ((), ())), preferred_element_type=F32
            )

        hidden[...] = lax.fori_loop(0, (stop - start) // size, sub, hidden[...])

    units(0, 3)
    pl.semaphore_wait(barrier, 22)
    core_copy(0).start()
    units(3, 4)
    scatter(0)
    units(4, 6)
    core_copy(1).start()
    units(6, 7)
    scatter(1)
    units(7, 9)
    core_copy(2).start()
    units(9, 10)
    scatter(2)
    units(10, 11)
    core_copy(3).start()
    units(11, 12)
    gather(0)
    units(12, 13)
    core_copy(4).start()
    scatter(3)
    gather(1)
    scatter(4)

    def pick_table():
        c = lax.broadcasted_iota(jnp.int32, (256, 128), 0)
        lane = lax.broadcasted_iota(jnp.int32, (256, 128), 1)
        inner = c & 31
        which = (c >> 5) * OWN + (inner >= 10).astype(jnp.int32) + (inner >= 20).astype(jnp.int32)
        which = jnp.where(inner < 30, which, -1000)
        for k in range(OWN):
            pick[k * 256 : (k + 1) * 256, :] = (lane == which + BINS * k).astype(F32).astype(BF16)

    pick_table()
    lab_row = label_v[:, 0:SNPS]
    counts = [
        jnp.sum((lab_row == first + k).astype(F32), axis=1, keepdims=True) for k in range(OWN)
    ]
    square_sums(0, 10240, 2560)
    gather(2)
    square_sums(10240, SNPS, 2560)
    share(0)
    gather(3)
    share(1)
    gather(4)
    for g in range(len(GROUPS)):
        apply(g)

    dense[...] = jnp.zeros_like(dense)
    for k in range(OWN):
        dense[PROBES * k : PROBES * (k + 1), :] = (
            hidden[16 * k : 16 * k + PROBES, :] / counts[k]
        )
    fields[pl.ds(bin_, 1)] = dense[...].astype(BF16)[None]
    for d in (4, 3, 5, 2, 6, 1, 7):
        pltpu.make_async_remote_copy(
            src_ref=fields.at[bin_], dst_ref=fields.at[bin_],
            send_sem=f_send.at[0], recv_sem=f_recv.at[0],
            device_id=(ind, lax.rem(bin_ + d, 8)), device_id_type=MESH,
        ).start()

    for k in range(OWN):
        field_out[:, k, :] = dense[PROBES * k : PROBES * (k + 1), :].astype(BF16)

    lane = lax.broadcasted_iota(jnp.int32, (128, 128), 1)
    extra = jnp.zeros((16, 128), F32)
    for k in range(OWN):
        extra = extra + split_dot(squares[k], (lane == 72 + k).astype(F32).astype(BF16))
        extra = extra + split_dot(quads[k], (lane == 75 + k).astype(F32).astype(BF16))
    extra = extra[0:8] + extra[8:16]

    seven_fields = fields.at[0:7]
    pltpu.make_async_copy(seven_fields, seven_fields, f_recv.at[0]).wait()
    own = fields[pl.ds(bin_, 1)].reshape(32, ROWS)
    every = fields[...].reshape(256, ROWS)
    gram = lax.dot_general(own, every, (((1,), (1,)), ((), ())), preferred_element_type=F32)
    r = lax.broadcasted_iota(jnp.int32, (32, 256), 0)
    c = lax.broadcasted_iota(jnp.int32, (32, 256), 1) & 31
    rk = (r >= 10).astype(jnp.int32) + (r >= 20).astype(jnp.int32)
    ck = (c >= 10).astype(jnp.int32) + (c >= 20).astype(jnp.int32)
    gram = jnp.where(r - 10 * rk == c - 10 * ck, gram, 0.0)
    by_bin = jnp.concatenate([jnp.where(rk == k, gram, 0.0) for k in range(OWN)], axis=1)
    pairs = split_dot(by_bin, pick[...])
    message = jnp.sum(jnp.sum(pairs.reshape(8, 8, 128), axis=0) + extra, axis=0, keepdims=True)
    messages[pl.ds(ind, 1)] = message[None]
    for d in (8, 7, 9, 6, 10, 5, 11, 4, 12, 3, 13, 2, 14, 1, 15):
        pltpu.make_async_remote_copy(
            src_ref=messages.at[ind], dst_ref=messages.at[ind],
            send_sem=m_send.at[0], recv_sem=m_recv.at[0],
            device_id=(lax.rem(ind + d, 16), bin_), device_id_type=MESH,
        ).start()

    for g in range(len(GROUPS)):
        core_copy(g).wait_send()
        pltpu.make_async_copy(all_slots(g), all_slots(g), rs_send.at[g]).wait()
        pltpu.make_async_copy(gathered(g), gathered(g), ag_send.at[g]).wait()
        if g not in DIRECT:
            half_copy(g).wait_send()
    pltpu.make_async_copy(seven_fields, seven_fields, f_send.at[0]).wait()

    fifteen = messages.at[0:15]
    pltpu.make_async_copy(fifteen, fifteen, m_recv.at[0]).wait()
    total = messages[0]
    for i in range(1, 16):
        total = total + messages[i]
    for k in range(OWN):
        pair_out[k : k + 1, :] = total[:, BINS * k : BINS * (k + 1)] / (PROBES * INDIVIDUALS)
        trace_out[:, k : k + 1] = total[:, 72 + k : 73 + k] / (counts[k] * INDIVIDUALS)
        quad_out[:, k : k + 1] = total[:, 75 + k : 76 + k] / (counts[k] * INDIVIDUALS)
    pltpu.make_async_copy(fifteen, fifteen, m_send.at[0]).wait()


def hand_over(*refs):
    for src, dst in zip(refs[:4], refs[4:]):
        dst[...] = src[...]


def shards(genotype, snp_mean, snp_scale, snp_label, probe_bits, phenotype):
    anywhere = pl.BlockSpec(memory_space=pl.ANY)
    vmem = pl.BlockSpec(memory_space=pltpu.VMEM)
    dma = pltpu.SemaphoreType.DMA
    n = len(GROUPS)
    shapes = (
        jax.ShapeDtypeStruct((PROBES, OWN, ROWS), BF16),
        jax.ShapeDtypeStruct((OWN, BINS), F32),
        jax.ShapeDtypeStruct((1, OWN), F32),
        jax.ShapeDtypeStruct((1, OWN), F32),
    )
    results = pl.pallas_call(
        kernel,
        name="moments_and_fields",
        out_shape=shapes,
        in_specs=[anywhere] * 6,
        out_specs=(vmem,) * 4,
        scratch_shapes=[
            pltpu.VMEM((ROWS, SNPS), jnp.int32),
            pltpu.VMEM((ROWS, SNPS), BF16),
            pltpu.VMEM((16, PADDED), F32),
            pltpu.VMEM((16, PADDED), F32),
            pltpu.VMEM((16, PADDED), BF16),
            pltpu.VMEM((7, 16, PADDED // 16), BF16),
            pltpu.VMEM((16, PADDED), BF16),
            pltpu.VMEM((1, SNPS), F32),
            pltpu.VMEM((1, SNPS), F32),
            pltpu.VMEM((1, PADDED), jnp.int32),
            pltpu.VMEM((PROBES, ROWS), jnp.int32),
            pltpu.VMEM((ROWS,), BF16),
            pltpu.VMEM((16, ROWS), F32),
            pltpu.VMEM((16, ROWS), BF16),
            pltpu.VMEM((OWN, 8, 128), F32),
            pltpu.VMEM((OWN, 8, 128), F32),
            pltpu.VMEM((16 * OWN, ROWS), F32),
            pltpu.VMEM((32, ROWS), F32),
            pltpu.VMEM((8, 32, ROWS), BF16),
            pltpu.VMEM((16, 1, 128), F32),
            pltpu.VMEM((768, 128), BF16),
            dma((UNITS,)), dma((5,)),
            dma((n,)), dma((n,)), dma((n,)), dma((n,)), dma((n,)), dma((n,)), dma((n,)), dma((n,)),
            dma((1,)), dma((1,)), dma((1,)), dma((1,)),
        ],
        compiler_params=pltpu.CompilerParams(
            collective_id=0, has_side_effects=True, vmem_limit_bytes=58 * 2**20
        ),
        cost_estimate=pl.CostEstimate(
            flops=2 * 64 * ROWS * SNPS, bytes_accessed=4 * ROWS * SNPS, transcendentals=0
        ),
    )(
        genotype,
        snp_mean.reshape(1, -1),
        snp_scale.reshape(1, -1),
        snp_label.reshape(1, -1),
        probe_bits,
        phenotype,
    )
    field, pair, trace, quad = pl.pallas_call(
        hand_over, name="hand_over", out_shape=shapes, in_specs=[vmem] * 4, out_specs=(vmem,) * 4
    )(*results)
    return field.transpose(1, 0, 2), pair, trace.reshape(-1), quad.reshape(-1)


def solution(mesh):
    placed = (P("ind", "bin"), P("bin"), P("bin"), P("bin"), P(None, "ind"), P("ind"))
    return jax.shard_map(
        shards,
        mesh=mesh,
        in_specs=placed,
        out_specs=(P("bin", None, "ind"), P("bin", None), P("bin"), P("bin")),
        check_vma=False,
    )
```

```python
import functools

import jax
import jax.numpy as jnp
from jax import lax
from jax.experimental import pallas as pl
from jax.experimental.pallas import tpu as pltpu
from jax.sharding import PartitionSpec as P

BINS = 24
PROBES = 10
OWN = 3
ROWS = 256
SNPS = 25600
INDIVIDUALS = 4096
UNIT = 2048
PADDED = 26624
UNITS = 13
AHEAD = 3
GROUPS = ((0, 3), (3, 3), (6, 3), (9, 2), (11, 2))
DIRECT = (2, 3, 4)
F32 = jnp.float32
BF16 = jnp.bfloat16
MESH = pl.DeviceIdType.MESH


def split_dot(a, b):
    high = a.astype(BF16)
    low = (a - high.astype(F32)).astype(BF16)
    both = jnp.concatenate([high, low], axis=0)
    return jnp.dot(both, b, preferred_element_type=F32)


def kernel(
    geno, mean, scale, label, probes, pheno,
    field_out, pair_out, trace_out, quad_out,
    gbuf, stand, part, other, sums, arrived, weights,
    mean_v, inv_v, label_v, probes_v, pheno_v, left_f, left_b, squares, quads, share_v, hidden, dense, fields, messages, pick,
    g_sem, s_sem, core_send, core_recv, rs_send, rs_recv, ag_send, ag_recv, half_send, half_recv,
    f_send, f_recv, m_send, m_recv,
):
    ind = lax.axis_index("ind")
    bin_ = lax.axis_index("bin")
    core = lax.rem(ind, 2)
    chip = ind // 2
    cx, cz = chip // 2, lax.rem(chip, 2)
    first = bin_ * OWN

    small = [
        pltpu.make_async_copy(mean, mean_v, s_sem.at[0]),
        pltpu.make_async_copy(scale, inv_v, s_sem.at[1]),
        pltpu.make_async_copy(label, label_v.at[:, 0:SNPS], s_sem.at[2]),
        pltpu.make_async_copy(probes, probes_v, s_sem.at[3]),
        pltpu.make_async_copy(pheno, pheno_v, s_sem.at[4]),
    ]
    for copy in small:
        copy.start()

    def geno_copy(u):
        at = pl.ds(pl.multiple_of(u * UNIT, UNIT), UNIT)
        return pltpu.make_async_copy(geno.at[:, at], gbuf.at[:, at], g_sem.at[u])

    last_at = pl.ds((UNITS - 1) * UNIT, SNPS - (UNITS - 1) * UNIT)
    last_copy = pltpu.make_async_copy(geno.at[:, last_at], gbuf.at[:, last_at], g_sem.at[UNITS - 1])
    for u in range(AHEAD):
        geno_copy(u).start()

    barrier = pltpu.get_barrier_semaphore()
    for d in range(1, 16):
        pl.semaphore_signal(
            barrier, inc=1, device_id=(lax.rem(ind + d, 16), bin_), device_id_type=MESH
        )
    for d in range(1, 8):
        pl.semaphore_signal(
            barrier, inc=1, device_id=(ind, lax.rem(bin_ + d, 8)), device_id_type=MESH
        )

    part[:, SNPS:PADDED] = jnp.zeros((16, PADDED - SNPS), F32)
    label_v[:, SNPS:PADDED] = jnp.full((1, PADDED - SNPS), -1, jnp.int32)
    squares[...] = jnp.zeros_like(squares)
    quads[...] = jnp.zeros_like(quads)
    hidden[...] = jnp.zeros_like(hidden)
    for copy in small:
        copy.wait()
    left_f[...] = jnp.zeros_like(left_f)
    left_f[0:PROBES, :] = (2 * probes_v[...] - 1).astype(F32)
    left_f[PROBES : PROBES + 1, :] = pheno_v[...].astype(F32).reshape(1, ROWS)
    left_b[...] = left_f[...].astype(BF16)
    inv_v[...] = 1.0 / inv_v[...]

    def fold(into, wide, lab):
        for k in range(OWN):
            own = jnp.where(lab == first + k, wide, 0.0)
            add = into[k]
            for t in range(own.shape[1] // 128):
                add = add + own[:, t * 128 : (t + 1) * 128]
            into[k] = add

    def moments(start, size):
        at = pl.ds(pl.multiple_of(start, size), size)
        x = ((gbuf[:, at].astype(F32) - mean_v[:, at]) * inv_v[:, at]).astype(BF16)
        stand[:, at] = x
        part[:, at] = jnp.dot(left_b[...], x, preferred_element_type=F32)

    def square_sums(lo, hi, size):
        def sub(s, _):
            at = pl.ds(pl.multiple_of(s * size, size), size)
            wide = stand[:, at].astype(F32)
            fold(squares, jnp.sum((wide * wide).reshape(ROWS // 8, 8, size), axis=0), label_v[:, at])
            return 0

        lax.fori_loop(lo // size, hi // size, sub, 0)

    def unit_moments(u, _):
        @pl.when(u + AHEAD < UNITS - 1)
        def _():
            geno_copy(u + AHEAD).start()

        @pl.when(u + AHEAD == UNITS - 1)
        def _():
            last_copy.start()

        geno_copy(u).wait()
        moments(u * UNIT, UNIT)
        return 0

    def units(lo, hi):
        lax.fori_loop(lo, min(hi, UNITS - 1), unit_moments, 0)
        if hi == UNITS:
            last_copy.wait()
            moments((UNITS - 1) * UNIT, SNPS - (UNITS - 1) * UNIT)

    def half_at(g, which):
        begin, n = GROUPS[g]
        half = n * UNIT // 2
        return pl.ds(pl.multiple_of(begin * UNIT + which * half, 1024), half)

    def piece_at(g, who):
        begin, n = GROUPS[g]
        half, piece = n * UNIT // 2, n * UNIT // 16
        return pl.ds(pl.multiple_of(begin * UNIT + core * half + who * piece, 128), piece)

    def partner():
        return (chip * 2 + 1 - core, bin_)

    def core_copy(g):
        at = half_at(g, 1 - core)
        return pltpu.make_async_remote_copy(
            src_ref=part.at[:, at], dst_ref=other.at[:, at],
            send_sem=core_send.at[g], recv_sem=core_recv.at[g],
            device_id=partner(), device_id_type=MESH,
        )

    hops = ((2, 1), (1, 1), (3, 1), (2, 0), (0, 1), (1, 0), (3, 0))

    def chip_at(hop):
        return lax.rem(cx + hop[0], 4) * 2 + lax.rem(cz + hop[1], 2)

    def slots(g):
        begin, n = GROUPS[g]
        return pl.ds(begin * 128, n * 128)

    def scatter(g):
        pltpu.make_async_copy(part.at[:, half_at(g, 1 - core)], other.at[:, half_at(g, core)], core_recv.at[g]).wait()
        at = half_at(g, core)
        sums[:, at] = (part[:, at] + other[:, at]).astype(BF16)
        for slot, hop in enumerate(hops):
            who = chip_at(hop)
            pltpu.make_async_remote_copy(
                src_ref=sums.at[:, piece_at(g, who)], dst_ref=arrived.at[slot, :, slots(g)],
                send_sem=rs_send.at[g], recv_sem=rs_recv.at[g],
                device_id=(who * 2 + core, bin_), device_id_type=MESH,
            ).start()

    def all_slots(g):
        return arrived.at[:, :, slots(g)]

    def gather(g):
        pltpu.make_async_copy(all_slots(g), all_slots(g), rs_recv.at[g]).wait()
        mine = piece_at(g, chip)
        total = part[:, mine] + other[:, mine]
        for slot in range(7):
            total = total + arrived[slot, :, slots(g)].astype(F32)
        weights[:, mine] = total.astype(BF16)
        targets = []
        for hop in hops:
            if g in DIRECT:
                targets.append(chip_at(hop) * 2 + 1 - core)
            targets.append(chip_at(hop) * 2 + core)
        if g in DIRECT:
            targets.append(chip * 2 + 1 - core)
        for target in targets:
            pltpu.make_async_remote_copy(
                src_ref=weights.at[:, mine], dst_ref=weights.at[:, mine],
                send_sem=ag_send.at[g], recv_sem=ag_recv.at[g],
                device_id=(target, bin_), device_id_type=MESH,
            ).start()
        trait = total[8:16, :]
        row = lax.broadcasted_iota(jnp.int32, trait.shape, 0)
        trait = jnp.where(row == PROBES - 8, trait * trait, 0.0)
        fold(quads, trait, label_v[:, mine])

    def gathered(g):
        begin, n = GROUPS[g]
        count = 15 if g in DIRECT else 7
        return weights.at[:, pl.ds(begin * UNIT, count * n * UNIT // 16)]

    def half_copy(g):
        at = half_at(g, core)
        return pltpu.make_async_remote_copy(
            src_ref=weights.at[:, at], dst_ref=weights.at[:, at],
            send_sem=half_send.at[g], recv_sem=half_recv.at[g],
            device_id=partner(), device_id_type=MESH,
        )

    def share(g):
        pltpu.make_async_copy(gathered(g), gathered(g), ag_recv.at[g]).wait()
        half_copy(g).start()

    def apply(g):
        if g in DIRECT:
            pltpu.make_async_copy(gathered(g), gathered(g), ag_recv.at[g]).wait()
        else:
            there = weights.at[:, half_at(g, 1 - core)]
            pltpu.make_async_copy(there, there, half_recv.at[g]).wait()
        begin, n = GROUPS[g]
        start = begin * UNIT
        stop = min(start + n * UNIT, SNPS)

        size = stop - start

        def sub(s, acc):
            at = pl.ds(pl.multiple_of(start + s * size, 1024), size)
            w = weights[:, at].astype(F32)
            lab = label_v[:, at]
            e = jnp.concatenate(
                [jnp.where(lab == first + k, w, 0.0).astype(BF16) for k in range(OWN)], axis=0
            )
            return acc + lax.dot_general(
                e, stand[:, at], (((1,), (1,)), ((), ())), preferred_element_type=F32
            )

        hidden[...] = lax.fori_loop(0, (stop - start) // size, sub, hidden[...])

    units(0, 3)
    pl.semaphore_wait(barrier, 22)
    core_copy(0).start()
    units(3, 4)
    scatter(0)
    units(4, 6)
    core_copy(1).start()
    units(6, 7)
    scatter(1)
    units(7, 9)
    core_copy(2).start()
    units(9, 10)
    scatter(2)
    units(10, 11)
    core_copy(3).start()
    units(11, 12)
    gather(0)
    units(12, 13)
    core_copy(4).start()
    scatter(3)
    gather(1)
    scatter(4)

    def pick_table():
        c = lax.broadcasted_iota(jnp.int32, (256, 128), 0)
        lane = lax.broadcasted_iota(jnp.int32, (256, 128), 1)
        inner = c & 31
        which = (c >> 5) * OWN + (inner >= 10).astype(jnp.int32) + (inner >= 20).astype(jnp.int32)
        which = jnp.where(inner < 30, which, -1000)
        for k in range(OWN):
            pick[k * 256 : (k + 1) * 256, :] = (lane == which + BINS * k).astype(F32).astype(BF16)

    pick_table()
    lab_row = label_v[:, 0:SNPS]
    for k in range(OWN):
        count = jnp.sum((lab_row == first + k).astype(F32), axis=1, keepdims=True)
        share_v[k : k + 1, :] = jnp.broadcast_to(1.0 / count, (1, 128))
    square_sums(0, 10240, 2560)
    gather(2)
    square_sums(10240, SNPS, 2560)
    share(0)
    gather(3)
    apply(0)
    share(1)
    gather(4)
    apply(1)
    apply(2)
    apply(3)
    apply(4)

    shares = [share_v[k : k + 1, 0:1] for k in range(OWN)]
    dense[...] = jnp.zeros_like(dense)
    for k in range(OWN):
        dense[PROBES * k : PROBES * (k + 1), :] = (
            hidden[16 * k : 16 * k + PROBES, :] * shares[k]
        )
    fields[pl.ds(bin_, 1)] = dense[...].astype(BF16)[None]
    bz, by = bin_ // 4, lax.rem(bin_, 4)
    for dz, dy in ((1, 2), (1, 1), (1, 3), (0, 2), (1, 0), (0, 1), (0, 3)):
        target = lax.rem(bz + dz, 2) * 4 + lax.rem(by + dy, 4)
        pltpu.make_async_remote_copy(
            src_ref=fields.at[bin_], dst_ref=fields.at[bin_],
            send_sem=f_send.at[0], recv_sem=f_recv.at[0],
            device_id=(ind, target), device_id_type=MESH,
        ).start()

    for k in range(OWN):
        field_out[:, k, :] = dense[PROBES * k : PROBES * (k + 1), :].astype(BF16)

    lane = lax.broadcasted_iota(jnp.int32, (128, 128), 1)
    extra = jnp.zeros((16, 128), F32)
    for k in range(OWN):
        extra = extra + split_dot(squares[k], (lane == 72 + k).astype(F32).astype(BF16))
        extra = extra + split_dot(quads[k], (lane == 75 + k).astype(F32).astype(BF16))
    extra = extra[0:8] + extra[8:16]

    lane = lax.broadcasted_iota(jnp.int32, (1, 128), 1)
    factors = jnp.full((1, 128), 1.0 / (PROBES * INDIVIDUALS), F32)
    for k in range(OWN):
        factors = jnp.where((lane == 72 + k) | (lane == 75 + k), shares[k] / INDIVIDUALS, factors)

    seven_fields = fields.at[0:7]
    pltpu.make_async_copy(seven_fields, seven_fields, f_recv.at[0]).wait()
    own = fields[pl.ds(bin_, 1)].reshape(32, ROWS)
    every = fields[...].reshape(256, ROWS)
    gram = lax.dot_general(own, every, (((1,), (1,)), ((), ())), preferred_element_type=F32)
    r = lax.broadcasted_iota(jnp.int32, (32, 256), 0)
    c = lax.broadcasted_iota(jnp.int32, (32, 256), 1) & 31
    rk = (r >= 10).astype(jnp.int32) + (r >= 20).astype(jnp.int32)
    ck = (c >= 10).astype(jnp.int32) + (c >= 20).astype(jnp.int32)
    gram = jnp.where(r - 10 * rk == c - 10 * ck, gram, 0.0)
    by_bin = jnp.concatenate([jnp.where(rk == k, gram, 0.0) for k in range(OWN)], axis=1)
    pairs = split_dot(by_bin, pick[...])
    message = jnp.sum(jnp.sum(pairs.reshape(8, 8, 128), axis=0) + extra, axis=0, keepdims=True)
    messages[pl.ds(ind, 1)] = message[None]
    others = [chip_at(hop) * 2 + c for hop in hops for c in (1 - core, core)]
    for target in others + [chip * 2 + 1 - core]:
        pltpu.make_async_remote_copy(
            src_ref=messages.at[ind], dst_ref=messages.at[ind],
            send_sem=m_send.at[0], recv_sem=m_recv.at[0],
            device_id=(target, bin_), device_id_type=MESH,
        ).start()

    for g in range(len(GROUPS)):
        core_copy(g).wait_send()
        pltpu.make_async_copy(all_slots(g), all_slots(g), rs_send.at[g]).wait()
        pltpu.make_async_copy(gathered(g), gathered(g), ag_send.at[g]).wait()
        if g not in DIRECT:
            half_copy(g).wait_send()
    pltpu.make_async_copy(seven_fields, seven_fields, f_send.at[0]).wait()

    fifteen = messages.at[0:15]
    pltpu.make_async_copy(fifteen, fifteen, m_recv.at[0]).wait()
    total = messages[0]
    for i in range(1, 16):
        total = total + messages[i]
    total = total * factors
    for k in range(OWN):
        pair_out[k : k + 1, :] = total[:, BINS * k : BINS * (k + 1)]
    trace_out[...] = total[:, 72 : 72 + OWN]
    quad_out[...] = total[:, 75 : 75 + OWN]
    pltpu.make_async_copy(fifteen, fifteen, m_send.at[0]).wait()


def hand_over(*refs):
    for src, dst in zip(refs[:4], refs[4:]):
        dst[...] = src[...]


def shards(genotype, snp_mean, snp_scale, snp_label, probe_bits, phenotype):
    anywhere = pl.BlockSpec(memory_space=pl.ANY)
    vmem = pl.BlockSpec(memory_space=pltpu.VMEM)
    dma = pltpu.SemaphoreType.DMA
    n = len(GROUPS)
    shapes = (
        jax.ShapeDtypeStruct((PROBES, OWN, ROWS), BF16),
        jax.ShapeDtypeStruct((OWN, BINS), F32),
        jax.ShapeDtypeStruct((1, OWN), F32),
        jax.ShapeDtypeStruct((1, OWN), F32),
    )
    results = pl.pallas_call(
        kernel,
        name="moments_and_fields",
        out_shape=shapes,
        in_specs=[anywhere] * 6,
        out_specs=(vmem,) * 4,
        scratch_shapes=[
            pltpu.VMEM((ROWS, SNPS), jnp.int32),
            pltpu.VMEM((ROWS, SNPS), BF16),
            pltpu.VMEM((16, PADDED), F32),
            pltpu.VMEM((16, PADDED), F32),
            pltpu.VMEM((16, PADDED), BF16),
            pltpu.VMEM((7, 16, PADDED // 16), BF16),
            pltpu.VMEM((16, PADDED), BF16),
            pltpu.VMEM((1, SNPS), F32),
            pltpu.VMEM((1, SNPS), F32),
            pltpu.VMEM((1, PADDED), jnp.int32),
            pltpu.VMEM((PROBES, ROWS), jnp.int32),
            pltpu.VMEM((ROWS,), BF16),
            pltpu.VMEM((16, ROWS), F32),
            pltpu.VMEM((16, ROWS), BF16),
            pltpu.VMEM((OWN, 8, 128), F32),
            pltpu.VMEM((OWN, 8, 128), F32),
            pltpu.VMEM((8, 128), F32),
            pltpu.VMEM((16 * OWN, ROWS), F32),
            pltpu.VMEM((32, ROWS), F32),
            pltpu.VMEM((8, 32, ROWS), BF16),
            pltpu.VMEM((16, 1, 128), F32),
            pltpu.VMEM((768, 128), BF16),
            dma((UNITS,)), dma((5,)),
            dma((n,)), dma((n,)), dma((n,)), dma((n,)), dma((n,)), dma((n,)), dma((n,)), dma((n,)),
            dma((1,)), dma((1,)), dma((1,)), dma((1,)),
        ],
        compiler_params=pltpu.CompilerParams(
            collective_id=0, has_side_effects=True, vmem_limit_bytes=58 * 2**20
        ),
        cost_estimate=pl.CostEstimate(
            flops=2 * 64 * ROWS * SNPS, bytes_accessed=4 * ROWS * SNPS, transcendentals=0
        ),
    )(
        genotype,
        snp_mean.reshape(1, -1),
        snp_scale.reshape(1, -1),
        snp_label.reshape(1, -1),
        probe_bits,
        phenotype,
    )
    field, pair, trace, quad = pl.pallas_call(
        hand_over, name="hand_over", out_shape=shapes, in_specs=[vmem] * 4, out_specs=(vmem,) * 4
    )(*results)
    return field.transpose(1, 0, 2), pair, trace.reshape(-1), quad.reshape(-1)


def solution(mesh):
    placed = (P("ind", "bin"), P("bin"), P("bin"), P("bin"), P(None, "ind"), P("ind"))
    return jax.shard_map(
        shards,
        mesh=mesh,
        in_specs=placed,
        out_specs=(P("bin", None, "ind"), P("bin", None), P("bin"), P("bin")),
        check_vma=False,
    )
```

```python
import functools

import jax
import jax.numpy as jnp
from jax import lax
from jax.experimental import pallas as pl
from jax.experimental.pallas import tpu as pltpu
from jax.sharding import PartitionSpec as P

BINS = 24
PROBES = 10
OWN = 3
ROWS = 256
SNPS = 25600
INDIVIDUALS = 4096
UNIT = 2048
PADDED = 26624
UNITS = 13
AHEAD = 4
GROUPS = ((0, 3), (3, 3), (6, 3), (9, 2), (11, 2))
DIRECT = (2, 3, 4)
F32 = jnp.float32
BF16 = jnp.bfloat16
MESH = pl.DeviceIdType.MESH


def split_dot(a, b):
    high = a.astype(BF16)
    low = (a - high.astype(F32)).astype(BF16)
    both = jnp.concatenate([high, low], axis=0)
    return jnp.dot(both, b, preferred_element_type=F32)


def kernel(
    geno, mean, scale, label, probes, pheno,
    field_out, row_out,
    gbuf, stand, part, other, sums, arrived, weights,
    mean_v, inv_v, label_v, probes_v, pheno_v, left_f, left_b, squares, quads, share_v, hidden, dense, fields, messages, pick, field_v,
    g_sem, s_sem, core_send, core_recv, rs_send, rs_recv, ag_send, ag_recv, half_send, half_recv,
    f_send, f_recv, m_send, m_recv, out_sem,
):
    ind = lax.axis_index("ind")
    bin_ = lax.axis_index("bin")
    core = lax.rem(ind, 2)
    chip = ind // 2
    cx, cz = chip // 2, lax.rem(chip, 2)
    first = bin_ * OWN

    small = [
        pltpu.make_async_copy(mean, mean_v, s_sem.at[0]),
        pltpu.make_async_copy(scale, inv_v, s_sem.at[1]),
        pltpu.make_async_copy(label, label_v.at[:, 0:SNPS], s_sem.at[2]),
        pltpu.make_async_copy(probes, probes_v, s_sem.at[3]),
        pltpu.make_async_copy(pheno, pheno_v, s_sem.at[4]),
    ]
    def geno_copy(u):
        at = pl.ds(pl.multiple_of(u * UNIT, UNIT), UNIT)
        return pltpu.make_async_copy(geno.at[:, at], gbuf.at[:, at], g_sem.at[u])

    last_at = pl.ds((UNITS - 1) * UNIT, SNPS - (UNITS - 1) * UNIT)
    last_copy = pltpu.make_async_copy(geno.at[:, last_at], gbuf.at[:, last_at], g_sem.at[UNITS - 1])
    for u in range(AHEAD):
        geno_copy(u).start(priority=1)
    for copy in small:
        copy.start()

    barrier = pltpu.get_barrier_semaphore()
    for d in range(1, 16):
        pl.semaphore_signal(
            barrier, inc=1, device_id=(lax.rem(ind + d, 16), bin_), device_id_type=MESH
        )
    for d in range(1, 8):
        pl.semaphore_signal(
            barrier, inc=1, device_id=(ind, lax.rem(bin_ + d, 8)), device_id_type=MESH
        )

    part[:, SNPS:PADDED] = jnp.zeros((16, PADDED - SNPS), F32)
    label_v[:, SNPS:PADDED] = jnp.full((1, PADDED - SNPS), -1, jnp.int32)
    squares[...] = jnp.zeros_like(squares)
    quads[...] = jnp.zeros_like(quads)
    hidden[...] = jnp.zeros_like(hidden)
    for copy in small:
        copy.wait()
    left_f[...] = jnp.zeros_like(left_f)
    left_f[0:PROBES, :] = (2 * probes_v[...] - 1).astype(F32)
    left_f[PROBES : PROBES + 1, :] = pheno_v[...].astype(F32).reshape(1, ROWS)
    left_b[...] = left_f[...].astype(BF16)
    inv_v[...] = 1.0 / inv_v[...]

    def fold(into, wide, lab):
        for k in range(OWN):
            own = jnp.where(lab == first + k, wide, 0.0)
            add = into[k]
            for t in range(own.shape[1] // 128):
                add = add + own[:, t * 128 : (t + 1) * 128]
            into[k] = add

    def moments(start, size):
        at = pl.ds(pl.multiple_of(start, size), size)
        x = ((gbuf[:, at].astype(F32) - mean_v[:, at]) * inv_v[:, at]).astype(BF16)
        stand[:, at] = x
        part[:, at] = jnp.dot(left_b[...], x, preferred_element_type=F32)

    def square_sums(lo, hi, size):
        def sub(s, _):
            at = pl.ds(pl.multiple_of(s * size, size), size)
            wide = stand[:, at].astype(F32)
            fold(squares, jnp.sum((wide * wide).reshape(ROWS // 8, 8, size), axis=0), label_v[:, at])
            return 0

        lax.fori_loop(lo // size, hi // size, sub, 0)

    def unit_moments(u, _):
        @pl.when(u + AHEAD < UNITS - 1)
        def _():
            geno_copy(u + AHEAD).start(priority=1)

        @pl.when(u + AHEAD == UNITS - 1)
        def _():
            last_copy.start(priority=1)

        geno_copy(u).wait()
        moments(u * UNIT, UNIT)
        return 0

    def units(lo, hi):
        lax.fori_loop(lo, min(hi, UNITS - 1), unit_moments, 0)
        if hi == UNITS:
            last_copy.wait()
            moments((UNITS - 1) * UNIT, SNPS - (UNITS - 1) * UNIT)

    def half_at(g, which):
        begin, n = GROUPS[g]
        half = n * UNIT // 2
        return pl.ds(pl.multiple_of(begin * UNIT + which * half, 1024), half)

    def piece_at(g, who):
        begin, n = GROUPS[g]
        half, piece = n * UNIT // 2, n * UNIT // 16
        return pl.ds(pl.multiple_of(begin * UNIT + core * half + who * piece, 128), piece)

    def partner():
        return (chip * 2 + 1 - core, bin_)

    def core_copy(g):
        at = half_at(g, 1 - core)
        return pltpu.make_async_remote_copy(
            src_ref=part.at[:, at], dst_ref=other.at[:, at],
            send_sem=core_send.at[g], recv_sem=core_recv.at[g],
            device_id=partner(), device_id_type=MESH,
        )

    hops = ((2, 1), (1, 1), (3, 1), (2, 0), (0, 1), (1, 0), (3, 0))

    def chip_at(hop):
        return lax.rem(cx + hop[0], 4) * 2 + lax.rem(cz + hop[1], 2)

    def slots(g):
        begin, n = GROUPS[g]
        return pl.ds(begin * 128, n * 128)

    def scatter(g):
        pltpu.make_async_copy(part.at[:, half_at(g, 1 - core)], other.at[:, half_at(g, core)], core_recv.at[g]).wait()
        at = half_at(g, core)
        sums[:, at] = (part[:, at] + other[:, at]).astype(BF16)
        for slot, hop in enumerate(hops):
            who = chip_at(hop)
            pltpu.make_async_remote_copy(
                src_ref=sums.at[:, piece_at(g, who)], dst_ref=arrived.at[slot, :, slots(g)],
                send_sem=rs_send.at[g], recv_sem=rs_recv.at[g],
                device_id=(who * 2 + core, bin_), device_id_type=MESH,
            ).start()

    def all_slots(g):
        return arrived.at[:, :, slots(g)]

    def gather(g):
        pltpu.make_async_copy(all_slots(g), all_slots(g), rs_recv.at[g]).wait()
        mine = piece_at(g, chip)
        total = part[:, mine] + other[:, mine]
        for slot in range(7):
            total = total + arrived[slot, :, slots(g)].astype(F32)
        weights[:, mine] = total.astype(BF16)
        targets = []
        for hop in hops:
            if g in DIRECT:
                targets.append(chip_at(hop) * 2 + 1 - core)
            targets.append(chip_at(hop) * 2 + core)
        if g in DIRECT:
            targets.append(chip * 2 + 1 - core)
        for target in targets:
            pltpu.make_async_remote_copy(
                src_ref=weights.at[:, mine], dst_ref=weights.at[:, mine],
                send_sem=ag_send.at[g], recv_sem=ag_recv.at[g],
                device_id=(target, bin_), device_id_type=MESH,
            ).start()
        trait = total[8:16, :]
        row = lax.broadcasted_iota(jnp.int32, trait.shape, 0)
        trait = jnp.where(row == PROBES - 8, trait * trait, 0.0)
        fold(quads, trait, label_v[:, mine])

    def gathered(g):
        begin, n = GROUPS[g]
        count = 15 if g in DIRECT else 7
        return weights.at[:, pl.ds(begin * UNIT, count * n * UNIT // 16)]

    def half_copy(g):
        at = half_at(g, core)
        return pltpu.make_async_remote_copy(
            src_ref=weights.at[:, at], dst_ref=weights.at[:, at],
            send_sem=half_send.at[g], recv_sem=half_recv.at[g],
            device_id=partner(), device_id_type=MESH,
        )

    def share(g):
        pltpu.make_async_copy(gathered(g), gathered(g), ag_recv.at[g]).wait()
        half_copy(g).start()

    def apply(g):
        if g in DIRECT:
            pltpu.make_async_copy(gathered(g), gathered(g), ag_recv.at[g]).wait()
        else:
            there = weights.at[:, half_at(g, 1 - core)]
            pltpu.make_async_copy(there, there, half_recv.at[g]).wait()
        begin, n = GROUPS[g]
        start = begin * UNIT
        stop = min(start + n * UNIT, SNPS)

        size = stop - start

        def sub(s, acc):
            at = pl.ds(pl.multiple_of(start + s * size, 1024), size)
            w = weights[:, at].astype(F32)
            lab = label_v[:, at]
            e = jnp.concatenate(
                [jnp.where(lab == first + k, w, 0.0).astype(BF16) for k in range(OWN)], axis=0
            )
            return acc + lax.dot_general(
                e, stand[:, at], (((1,), (1,)), ((), ())), preferred_element_type=F32
            )

        hidden[...] = lax.fori_loop(0, (stop - start) // size, sub, hidden[...])

    units(0, 3)
    pl.semaphore_wait(barrier, 22)
    core_copy(0).start()
    units(3, 4)
    scatter(0)
    units(4, 6)
    core_copy(1).start()
    units(6, 7)
    scatter(1)
    units(7, 9)
    core_copy(2).start()
    units(9, 10)
    scatter(2)
    units(10, 11)
    core_copy(3).start()
    units(11, 12)
    gather(0)
    units(12, 13)
    core_copy(4).start()
    scatter(3)
    gather(1)
    scatter(4)

    def pick_table():
        c = lax.broadcasted_iota(jnp.int32, (256, 128), 0)
        lane = lax.broadcasted_iota(jnp.int32, (256, 128), 1)
        inner = c & 31
        which = (c >> 5) * OWN + (inner >= 10).astype(jnp.int32) + (inner >= 20).astype(jnp.int32)
        which = jnp.where(inner < 30, which, -1000)
        for k in range(OWN):
            pick[k * 256 : (k + 1) * 256, :] = (lane == which + BINS * k).astype(F32).astype(BF16)

    pick_table()
    lab_row = label_v[:, 0:SNPS]
    for k in range(OWN):
        count = jnp.sum((lab_row == first + k).astype(F32), axis=1, keepdims=True)
        share_v[k : k + 1, :] = jnp.broadcast_to(1.0 / count, (1, 128))
    square_sums(0, 10240, 2560)
    gather(2)
    square_sums(10240, SNPS, 2560)
    share(0)
    gather(3)
    apply(0)
    share(1)
    gather(4)
    apply(1)
    apply(2)
    apply(3)
    apply(4)

    shares = [share_v[k : k + 1, 0:1] for k in range(OWN)]
    dense[...] = jnp.zeros_like(dense)
    for k in range(OWN):
        dense[PROBES * k : PROBES * (k + 1), :] = (
            hidden[16 * k : 16 * k + PROBES, :] * shares[k]
        )
    fields[pl.ds(bin_, 1)] = dense[...].astype(BF16)[None]
    bz, by = bin_ // 4, lax.rem(bin_, 4)
    for dz, dy in ((1, 2), (1, 1), (1, 3), (0, 2), (1, 0), (0, 1), (0, 3)):
        target = lax.rem(bz + dz, 2) * 4 + lax.rem(by + dy, 4)
        pltpu.make_async_remote_copy(
            src_ref=fields.at[bin_], dst_ref=fields.at[bin_],
            send_sem=f_send.at[0], recv_sem=f_recv.at[0],
            device_id=(ind, target), device_id_type=MESH,
        ).start()

    for k in range(OWN):
        field_v[:, k, :] = dense[PROBES * k : PROBES * (k + 1), :].astype(BF16)
    field_copy = pltpu.make_async_copy(field_v, field_out, out_sem.at[0])
    field_copy.start()

    lane = lax.broadcasted_iota(jnp.int32, (128, 128), 1)
    extra = jnp.zeros((16, 128), F32)
    for k in range(OWN):
        extra = extra + split_dot(squares[k], (lane == 72 + k).astype(F32).astype(BF16))
        extra = extra + split_dot(quads[k], (lane == 75 + k).astype(F32).astype(BF16))
    extra = extra[0:8] + extra[8:16]

    lane = lax.broadcasted_iota(jnp.int32, (1, 128), 1)
    factors = jnp.full((1, 128), 1.0 / (PROBES * INDIVIDUALS), F32)
    for k in range(OWN):
        factors = jnp.where((lane == 72 + k) | (lane == 75 + k), shares[k] / INDIVIDUALS, factors)

    seven_fields = fields.at[0:7]
    pltpu.make_async_copy(seven_fields, seven_fields, f_recv.at[0]).wait()
    own = fields[pl.ds(bin_, 1)].reshape(32, ROWS)
    every = fields[...].reshape(256, ROWS)
    gram = lax.dot_general(own, every, (((1,), (1,)), ((), ())), preferred_element_type=F32)
    r = lax.broadcasted_iota(jnp.int32, (32, 256), 0)
    c = lax.broadcasted_iota(jnp.int32, (32, 256), 1) & 31
    rk = (r >= 10).astype(jnp.int32) + (r >= 20).astype(jnp.int32)
    ck = (c >= 10).astype(jnp.int32) + (c >= 20).astype(jnp.int32)
    gram = jnp.where(r - 10 * rk == c - 10 * ck, gram, 0.0)
    by_bin = jnp.concatenate([jnp.where(rk == k, gram, 0.0) for k in range(OWN)], axis=1)
    pairs = split_dot(by_bin, pick[...])
    message = jnp.sum(jnp.sum(pairs.reshape(8, 8, 128), axis=0) + extra, axis=0, keepdims=True)
    messages[pl.ds(ind, 1)] = message[None]
    others = [chip_at(hop) * 2 + c for hop in hops for c in (1 - core, core)]
    for target in others + [chip * 2 + 1 - core]:
        pltpu.make_async_remote_copy(
            src_ref=messages.at[ind], dst_ref=messages.at[ind],
            send_sem=m_send.at[0], recv_sem=m_recv.at[0],
            device_id=(target, bin_), device_id_type=MESH,
        ).start()

    for g in range(len(GROUPS)):
        core_copy(g).wait_send()
        pltpu.make_async_copy(all_slots(g), all_slots(g), rs_send.at[g]).wait()
        pltpu.make_async_copy(gathered(g), gathered(g), ag_send.at[g]).wait()
        if g not in DIRECT:
            half_copy(g).wait_send()
    pltpu.make_async_copy(seven_fields, seven_fields, f_send.at[0]).wait()

    fifteen = messages.at[0:15]
    pltpu.make_async_copy(fifteen, fifteen, m_recv.at[0]).wait()
    total = messages[0]
    for i in range(1, 16):
        total = total + messages[i]
    row_out[...] = total * factors
    field_copy.wait()
    pltpu.make_async_copy(fifteen, fifteen, m_send.at[0]).wait()


def hand_over(field, row, field_out, pair_out, trace_out, quad_out):
    field_out[...] = field[...]
    for k in range(OWN):
        pair_out[k : k + 1, :] = row[:, BINS * k : BINS * (k + 1)]
    trace_out[...] = row[:, 72 : 72 + OWN]
    quad_out[...] = row[:, 75 : 75 + OWN]


def shards(genotype, snp_mean, snp_scale, snp_label, probe_bits, phenotype):
    anywhere = pl.BlockSpec(memory_space=pl.ANY)
    vmem = pl.BlockSpec(memory_space=pltpu.VMEM)
    dma = pltpu.SemaphoreType.DMA
    n = len(GROUPS)
    shapes = (
        jax.ShapeDtypeStruct((PROBES, OWN, ROWS), BF16),
        jax.ShapeDtypeStruct((OWN, BINS), F32),
        jax.ShapeDtypeStruct((1, OWN), F32),
        jax.ShapeDtypeStruct((1, OWN), F32),
    )
    results = pl.pallas_call(
        kernel,
        name="moments_and_fields",
        out_shape=(shapes[0], jax.ShapeDtypeStruct((1, 128), F32)),
        in_specs=[anywhere] * 6,
        out_specs=(anywhere, vmem),
        scratch_shapes=[
            pltpu.VMEM((ROWS, SNPS), jnp.int32),
            pltpu.VMEM((ROWS, SNPS), BF16),
            pltpu.VMEM((16, PADDED), F32),
            pltpu.VMEM((16, PADDED), F32),
            pltpu.VMEM((16, PADDED), BF16),
            pltpu.VMEM((7, 16, PADDED // 16), BF16),
            pltpu.VMEM((16, PADDED), BF16),
            pltpu.VMEM((1, SNPS), F32),
            pltpu.VMEM((1, SNPS), F32),
            pltpu.VMEM((1, PADDED), jnp.int32),
            pltpu.VMEM((PROBES, ROWS), jnp.int32),
            pltpu.VMEM((ROWS,), BF16),
            pltpu.VMEM((16, ROWS), F32),
            pltpu.VMEM((16, ROWS), BF16),
            pltpu.VMEM((OWN, 8, 128), F32),
            pltpu.VMEM((OWN, 8, 128), F32),
            pltpu.VMEM((8, 128), F32),
            pltpu.VMEM((16 * OWN, ROWS), F32),
            pltpu.VMEM((32, ROWS), F32),
            pltpu.VMEM((8, 32, ROWS), BF16),
            pltpu.VMEM((16, 1, 128), F32),
            pltpu.VMEM((768, 128), BF16),
            pltpu.VMEM((PROBES, OWN, ROWS), BF16),
            dma((UNITS,)), dma((5,)),
            dma((n,)), dma((n,)), dma((n,)), dma((n,)), dma((n,)), dma((n,)), dma((n,)), dma((n,)),
            dma((1,)), dma((1,)), dma((1,)), dma((1,)), dma((1,)),
        ],
        compiler_params=pltpu.CompilerParams(
            collective_id=0, has_side_effects=True, vmem_limit_bytes=58 * 2**20
        ),
        cost_estimate=pl.CostEstimate(
            flops=2 * 64 * ROWS * SNPS, bytes_accessed=4 * ROWS * SNPS, transcendentals=0
        ),
    )(
        genotype,
        snp_mean.reshape(1, -1),
        snp_scale.reshape(1, -1),
        snp_label.reshape(1, -1),
        probe_bits,
        phenotype,
    )
    field, pair, trace, quad = pl.pallas_call(
        hand_over, name="hand_over", out_shape=shapes, in_specs=[vmem] * 2, out_specs=(vmem,) * 4
    )(*results)
    return field.transpose(1, 0, 2), pair, trace.reshape(-1), quad.reshape(-1)


def solution(mesh):
    placed = (P("ind", "bin"), P("bin"), P("bin"), P("bin"), P(None, "ind"), P("ind"))
    return jax.shard_map(
        shards,
        mesh=mesh,
        in_specs=placed,
        out_specs=(P("bin", None, "ind"), P("bin", None), P("bin"), P("bin")),
        check_vma=False,
    )
```
